256 devices in a mesh: expert: 16 (over x_lo, y, core), hidden: 16 (over z, x_hi).
Axes of the slice: x: 4 (x_hi: 2, x_lo: 2; x = x_hi * 2 + x_lo), y: 4, z: 8, core: 2. Of those that a mesh axis runs over, the one named last changes fastest.
Arguments:
- tokens: bfloat16 [4096, 7168], P('expert', 'hidden'), may hold values from -6 to 6
- route_ids: int32 [4096, 2], P('expert'), may hold values from 0 to 15, all different within a row; in each aligned block of 256 rows (0 to 255, 256 to 511, ...) at most 40 rows name the same one
- route_weight: float32 [4096, 2], P('expert'), may hold values from 0.2 to 2
- w_gate: bfloat16 [16, 7168, 2048], P('expert', None, 'hidden'), may hold values from -0.0625 to 0.0625
- w_up: bfloat16 [16, 7168, 2048], P('expert', None, 'hidden'), may hold values from -0.0625 to 0.0625
- w_down: bfloat16 [16, 2048, 7168], P('expert', 'hidden'), may hold values from -0.125 to 0.125
Outputs:
- mixed: bfloat16 [4096, 7168], P('expert', 'hidden')
The draws below stay inside these ranges and needn't reach their ends.
Inputs may be any that keep to these rules, and one draw needn't show every extreme that they name: `route_ids`: each row names 2 different experts. In the aligned blocks of 256 rows, no expert is named by more than 40 rows of one block, a bound that some block reaches.
All inputs are finite; a program needn't handle non-finite values.
Results may differ from the reference program's by a relative error of at most 0.0057.
Values may be sent and summed in bfloat16 or wider, within the bound.
No kernel may reach another device: no remote copies, remote signals or barrier semaphores. Data moves between devices by JAX's collectives and lax.ppermute only.
A program may use at most 128 MiB of HBM per device.

```python
import math
import jax
import jax.numpy as jnp
import numpy as np
from jax import lax

D = 7168
FF = 2048
TOK_DEV = 256
TOP = 2
CAP = 40
EXPERTS = 16
TOKENS = 4096
N_EXPERT = 16


def block_scale(key, dims, shards, low, high):
    level, own = 1.0, jax.random.fold_in(key, 6)
    for position, parts in shards:
        steps = jnp.exp(jax.random.uniform(jax.random.fold_in(own, position), (parts,), jnp.float32, low / len(shards), high / len(shards)))
        level = level * jnp.repeat(steps, dims[position] // parts).reshape([-1 if axis == position else 1 for axis in range(len(dims))])
    return level


def deal_out(stream_key, own, number, rows, number_of, top, reach, slope):
    sequence = jax.random.permutation(stream_key, number_of)
    crowded, usual = shares(number_of, rows * top, reach, slope, True), shares(number_of, rows * top, reach, slope, False)
    places = jnp.arange(number_of)

    def named(tallies, rotation):
        used = int((tallies > 0).sum())
        fixed = max(1, used // 4)
        passed = fixed + (places - fixed + rotation * (used - fixed)) % max(1, number_of - fixed)
        return jnp.zeros((number_of,), jnp.int32).at[sequence[jnp.where(places < fixed, places, passed)]].set(jnp.asarray(tallies, jnp.int32))

    tallies = jnp.where(number % 4 == 0, named(crowded, number // 4), named(usual, number - number // 4 - 1))
    mixed = jax.random.permutation(jax.random.fold_in(own, 3), number_of)
    giver, taker = mixed[0:number_of // 2 * 2:2], mixed[1:number_of // 2 * 2:2]
    margin = jnp.minimum(tallies[giver] - 1, reach - tallies[taker]) // 2
    margin = jnp.where((giver == sequence[0]) | (taker == sequence[0]) | (tallies[taker] == 0), 0, jnp.maximum(margin, 0))
    passed = jax.random.randint(jax.random.fold_in(own, 4), (number_of // 2,), 0, 1 << 20) % (margin + 1)
    tallies = tallies.at[giver].add(-passed).at[taker].add(passed)
    labels = jnp.searchsorted(jnp.cumsum(tallies), jnp.arange(rows * top), side="right").astype(jnp.int32)
    table = labels.reshape(top, rows).T
    table = table[jax.random.permutation(jax.random.fold_in(own, 1), rows)]
    rotation = jax.random.randint(jax.random.fold_in(own, 2), (rows, 1), 0, top)
    return jnp.take_along_axis(table, (jnp.arange(top)[None, :] + rotation) % top, axis=1)


def shares(amount, total, most, skew, full):
    weights = [(1 << 20) // math.isqrt(rank ** skew) + 1 for rank in range(1, amount + 1)]
    largest = most if full else min(most, max(-(-total // amount), total * weights[0] // sum(weights)))
    least = 1 if total - largest >= amount - 1 else 0
    given, rest = [largest] + [least] * (amount - 1), total - largest - least * (amount - 1)
    while rest > 0:
        candidates = [i for i in range(1, amount) if given[i] < largest] or [i for i in range(1, amount) if given[i] < most]
        whole, remaining = sum([weights[i] for i in candidates]), rest
        for i in candidates:
            addition = min(most - given[i], max(1, remaining * weights[i] // whole), rest)
            given[i] = given[i] + addition
            rest = rest - addition
    return np.array(given)


def bell_draw(stream_key, extent, width, most, cuts=(), kind=jnp.bfloat16):
    level = block_scale(stream_key, extent, cuts, -0.22, 0.18) if cuts else 1.0
    values = jax.random.normal(stream_key, extent, jnp.float32) * width * level
    return jnp.minimum(jnp.maximum(values, -most), most).astype(kind)


def setup_inputs(seed: int = 0) -> dict:
    key_of = jax.random.split(jax.random.key(seed), 7)
    tokens = bell_draw(key_of[0], (TOKENS, D), 1.0, 6.0, ((0, 16), (1, 16)))
    route_ids_keys = jax.random.split(jax.random.fold_in(key_of[1], 1), TOKENS // TOK_DEV)
    route_ids_turns = jax.random.permutation(jax.random.fold_in(key_of[1], 3), TOKENS // TOK_DEV)
    route_ids = jax.vmap(lambda own, number: deal_out(jax.random.fold_in(key_of[1], 2), own, number, TOK_DEV, EXPERTS, TOP, CAP, 2))(route_ids_keys, route_ids_turns).reshape((TOKENS, TOP))
    route_weight = jnp.clip(jnp.exp(math.log(2.0) - 2.3025851 * jax.random.uniform(key_of[2], (TOKENS, TOP), jnp.float32) ** block_scale(key_of[2], (TOKENS, TOP), ((0, 16),), -0.2, 0.2)), 0.2, 2.0)
    w_gate = bell_draw(key_of[3], (EXPERTS, D, FF), D ** -0.5, 0.0625, ((0, 16), (2, 16)))
    w_up = bell_draw(key_of[4], (EXPERTS, D, FF), D ** -0.5, 0.0625, ((0, 16), (2, 16)))
    w_down = bell_draw(key_of[5], (EXPERTS, FF, D), FF ** -0.5, 0.125, ((0, 16), (1, 16)))
    return dict(tokens=tokens, route_ids=route_ids, route_weight=route_weight, w_gate=w_gate, w_up=w_up, w_down=w_down)


def reference(tokens, route_ids, route_weight, w_gate, w_up, w_down):
    row_bound = N_EXPERT * CAP

    def advance(running, stacked):
        expert, gate_w, up_w, down_w = stacked
        matched = route_ids == expert
        chosen = jnp.any(matched, axis=1)
        weighting = jnp.sum(jnp.where(matched, route_weight, jnp.float32(0.0)), axis=1)
        row_index = jnp.nonzero(chosen, size=row_bound, fill_value=0)[0].astype(jnp.int32)
        is_live = jnp.arange(row_bound) < jnp.sum(chosen.astype(jnp.int32))
        picked = jnp.take(tokens, row_index, axis=0)
        gate_pre = jnp.dot(picked, gate_w, preferred_element_type=jnp.float32)
        up_pre = jnp.dot(picked, up_w, preferred_element_type=jnp.float32)
        hidden = (jax.nn.silu(gate_pre) * up_pre).astype(jnp.bfloat16)
        result = jnp.dot(hidden, down_w, preferred_element_type=jnp.float32).astype(jnp.bfloat16)
        result = lax.optimization_barrier(result).astype(jnp.float32)
        factor = jnp.where(is_live, jnp.take(weighting, row_index), jnp.float32(0.0))
        running = running.at[row_index].add(factor[:, None] * result)
        return running, None

    start_sum = jnp.zeros(tokens.shape, jnp.float32)
    running, _ = lax.scan(advance, start_sum, (jnp.arange(EXPERTS, dtype=jnp.int32), w_gate, w_up, w_down))
    return running.astype(jnp.bfloat16)
```

```python
import jax
import jax.numpy as jnp
from jax import lax
from jax.sharding import PartitionSpec as P

TOP = 2


def on_device(tokens, route_ids, route_weight, w_gate, w_up, w_down):
    experts = lax.axis_size("expert")
    parts = lax.axis_size("hidden")
    rows_dev, width = tokens.shape
    capacity = (rows_dev * TOP * 5 + 4 * experts - 1) // (4 * experts)
    slot_count = experts * capacity

    matches = route_ids[:, :, None] == jnp.arange(experts, dtype=jnp.int32)[None, None, :]
    chosen = jnp.any(matches, axis=1)
    before = jnp.arange(rows_dev)[:, None] > jnp.arange(rows_dev)[None, :]
    ranking = jnp.dot(
        before.astype(jnp.bfloat16), chosen.astype(jnp.bfloat16), preferred_element_type=jnp.float32
    )
    slot_of = jnp.arange(experts, dtype=jnp.float32)[None, :] * capacity + ranking
    slot_k = jnp.sum(jnp.where(matches, slot_of[:, None, :], 0.0), axis=2).astype(jnp.int32)
    slots = jnp.arange(slot_count, dtype=jnp.int32)
    picks_k = [slot_k[:, k][:, None] == slots[None, :] for k in range(TOP)]
    picks = (picks_k[0] | picks_k[1]).astype(jnp.bfloat16)

    down_w = lax.all_to_all(w_down[0], "hidden", split_axis=1, concat_axis=0, tiled=True)

    leaving = lax.dot_general(
        picks, tokens, (((0,), (0,)), ((), ())), preferred_element_type=jnp.float32
    ).astype(jnp.bfloat16)
    arrived = lax.all_to_all(
        leaving.reshape(experts, capacity, width), "expert", split_axis=0, concat_axis=0, tiled=True
    ).reshape(slot_count, width)
    rows = lax.all_gather(arrived, "hidden", axis=1, tiled=True)
    gate_sum = jnp.dot(rows, w_gate[0], preferred_element_type=jnp.float32)
    up_sum = jnp.dot(rows, w_up[0], preferred_element_type=jnp.float32)
    hidden = (jax.nn.silu(gate_sum) * up_sum).astype(jnp.bfloat16)
    every_hidden = lax.all_gather(hidden, "hidden", axis=1, tiled=True)
    produced = jnp.dot(every_hidden, down_w, preferred_element_type=jnp.float32).astype(jnp.bfloat16)
    returned = lax.all_to_all(
        produced.reshape(experts, capacity, width), "expert", split_axis=0, concat_axis=0, tiled=True
    ).reshape(slot_count, width)
    mixed = jnp.zeros((rows_dev, width), jnp.float32)
    for k in range(TOP):
        result = jnp.dot(
            picks_k[k].astype(jnp.bfloat16), returned, preferred_element_type=jnp.float32
        )
        mixed = mixed + route_weight[:, k][:, None] * result
    return mixed.astype(jnp.bfloat16)


def solution(mesh):
    in_specs = (
        P("expert", "hidden"),
        P("expert", None),
        P("expert", None),
        P("expert", None, "hidden"),
        P("expert", None, "hidden"),
        P("expert", "hidden", None),
    )
    out_specs = P("expert", "hidden")
    return jax.shard_map(
        on_device, mesh=mesh, in_specs=in_specs, out_specs=out_specs, check_vma=False
    )
```

```python
import jax
import jax.numpy as jnp
from jax import lax
from jax.experimental import pallas as pl
from jax.experimental.pallas import tpu as pltpu
from jax.sharding import Mesh, PartitionSpec as P

TOP = 2
SHAPE = (2, 4, 2, 8, 2)
NAMES = ("xl", "y", "core", "z", "xh")
PLANE = ("xl", "y", "xh")


def along_z(x, step):
    n = lax.axis_size("z")
    return lax.ppermute(x, "z", [(s, (s + step) % n) for s in range(n)])


def from_swapped(x):
    return lax.ppermute(x, ("core", "xh"), [(1, 2), (2, 1)])


def after(x, *others):
    return lax.optimization_barrier((x, others))[0]


def other_core(x):
    return lax.ppermute(x, "core", [(0, 1), (1, 0)])


def gate_up_body(tops, counts, first, last, units, *refs):
    n = len(counts)
    held, refs = refs[: len(tops)], refs[len(tops) :]
    weights, refs = refs[:2], refs[2:]
    before_ref, (out_ref, total) = (None, refs) if first else (refs[0], refs[1:])
    step = pl.program_id(0)

    @pl.when(step == 0)
    def _():
        total[...] = jnp.zeros_like(total) if first else before_ref[...]

    taken = 0
    for k in range(n):
        parts = [(held[j], tops[j]) for j in range(taken, taken + counts[k])]
        taken += counts[k]

        @pl.when(step == k)
        def _():
            w = jnp.concatenate([w_ref[...] for w_ref in weights], axis=1)
            for x_ref, top in parts:
                at = pl.ds(top, x_ref.shape[0])
                total[at, :] += jnp.dot(x_ref[...], w, preferred_element_type=jnp.float32)

    @pl.when(step == n - 1)
    def _():
        if not last:
            out_ref[...] = total[...]
            return
        for j in range(2):
            gate = total[:, 2 * j * units : (2 * j + 1) * units]
            up = total[:, (2 * j + 1) * units : (2 * j + 2) * units]
            act = gate / (1.0 + jnp.exp(-gate)) * up
            out_ref[:, j * units : (j + 1) * units] = act.astype(jnp.bfloat16)


def gate_up(blocks, weights, before=None, last=False):
    held = [x for parts in blocks for x, _ in parts]
    tops = [top for parts in blocks for _, top in parts]
    counts = [len(parts) for parts in blocks]
    n = len(blocks)
    units = weights[0].shape[1] // 2
    depth = held[0].shape[1]
    rows = sum(x.shape[0] for x, _ in blocks[0])
    whole = pl.BlockSpec(memory_space=pltpu.VMEM)
    w_spec = pl.BlockSpec((depth, 2 * units), lambda k: (k, 0))
    out = (rows, 2 * units) if last else (rows, 4 * units)
    return pl.pallas_call(
        lambda *refs: gate_up_body(tops, counts, before is None, last, units, *refs),
        grid=(n,),
        in_specs=[whole] * len(held) + [w_spec] * 2 + ([] if before is None else [whole]),
        out_specs=pl.BlockSpec(out, lambda k: (0, 0)),
        scratch_shapes=[pltpu.VMEM((rows, 4 * units), jnp.float32)],
        out_shape=jax.ShapeDtypeStruct(out, jnp.bfloat16 if last else jnp.float32),
        compiler_params=pltpu.CompilerParams(vmem_limit_bytes=24 << 20),
        cost_estimate=pl.CostEstimate(
            flops=8 * n * rows * depth * units,
            bytes_accessed=2 * n * depth * (rows + 4 * units),
            transcendentals=2 * rows * units if last else 0,
        ),
    )(*held, *weights, *([] if before is None else [before]))


def pack_gate_up_body(units, at_ref, gate_ref, up_ref, out_ref):
    out_ref[:, :units] = gate_ref[...]
    out_ref[:, units:] = up_ref[...]


def pack_gate_up(at, gate, up, depth):
    n, units = at.shape[0], gate.shape[1]
    spec = pl.BlockSpec((depth, units), lambda k, at_ref: (at_ref[k], 0))
    return pl.pallas_call(
        lambda *refs: pack_gate_up_body(units, *refs),
        grid_spec=pltpu.PrefetchScalarGridSpec(
            num_scalar_prefetch=1,
            grid=(n,),
            in_specs=[spec, spec],
            out_specs=pl.BlockSpec((depth, 2 * units), lambda k, at_ref: (k, 0)),
        ),
        out_shape=jax.ShapeDtypeStruct((n * depth, 2 * units), jnp.bfloat16),
        cost_estimate=pl.CostEstimate(
            flops=0, bytes_accessed=8 * n * depth * units, transcendentals=0
        ),
    )(at, gate, up)


def pack_down_body(at_ref, down_ref, out_ref):
    out_ref[0] = down_ref[...]


def pack_down(at, down, width):
    n, units = at.shape[0], down.shape[0]
    return pl.pallas_call(
        pack_down_body,
        grid_spec=pltpu.PrefetchScalarGridSpec(
            num_scalar_prefetch=1,
            grid=(n,),
            in_specs=[pl.BlockSpec((units, width), lambda k, at_ref: (0, at_ref[k]))],
            out_specs=pl.BlockSpec((1, units, width), lambda k, at_ref: (k, 0, 0)),
        ),
        out_shape=jax.ShapeDtypeStruct((n, units, width), jnp.bfloat16),
        cost_estimate=pl.CostEstimate(
            flops=0, bytes_accessed=4 * n * width * units, transcendentals=0
        ),
    )(at, down)


def on_device(tokens, route_ids, route_weight, w_gate, w_up, w_down):
    rows_dev, width = tokens.shape
    experts = lax.axis_size(PLANE)
    nz = lax.axis_size("z")
    z = lax.axis_index("z")
    capacity = (rows_dev * TOP * 5 + 4 * experts - 1) // (4 * experts)
    slot_count = experts * capacity
    owners = experts // 2
    units = w_gate.shape[2]

    matches = route_ids[:, :, None] == jnp.arange(experts, dtype=jnp.int32)[None, None, :]
    chosen = jnp.any(matches, axis=1)
    before = jnp.arange(rows_dev)[:, None] > jnp.arange(rows_dev)[None, :]
    ranking = jnp.dot(
        before.astype(jnp.bfloat16), chosen.astype(jnp.bfloat16), preferred_element_type=jnp.float32
    )
    slot_of = jnp.arange(experts, dtype=jnp.float32)[None, :] * capacity + ranking
    slot_k = jnp.sum(jnp.where(matches, slot_of[:, None, :], 0.0), axis=2).astype(jnp.int32)
    slots = jnp.arange(slot_count, dtype=jnp.int32)
    picks_k = [slot_k[:, k][:, None] == slots[None, :] for k in range(TOP)]
    picks = (picks_k[0] | picks_k[1]).astype(jnp.bfloat16)

    leaving = lax.dot_general(
        picks, tokens, (((0,), (0,)), ((), ())), preferred_element_type=jnp.float32
    ).astype(jnp.bfloat16)
    arrived = lax.all_to_all(
        leaving.reshape(experts, capacity, width), PLANE, split_axis=0, concat_axis=0, tiled=True
    )
    def at(places):
        return jnp.stack([(z + k) % nz for k in places]).astype(jnp.int32)

    def pick(mine, came):
        return jnp.where(lax.axis_index("core") == lax.axis_index("xh"), mine, came)

    mid = nz // 2
    near = list(range(mid - 1)) + list(range(2 - mid, 0))
    rest = [mid - 1, 1 - mid, mid]
    near_gu = pack_gate_up(at([-k for k in near]), w_gate[0], w_up[0], 2 * width)
    rest_gu = pack_gate_up(at([-k for k in rest]), w_gate[0], w_up[0], 2 * width)
    early_down = pack_down(at(rest), w_down[0], 2 * width)
    late_down = pack_down(at(near), w_down[0], 2 * width)
    arrived, near_gu, rest_gu = lax.optimization_barrier((arrived, near_gu, rest_gu))
    near_came = from_swapped(near_gu)

    half = owners // 2 * capacity
    rows = [
        part.transpose(0, 2, 1, 3).reshape(half, 2 * width)
        for part in jnp.split(arrived.reshape(owners, 2, capacity, width), 2)
    ]
    ups, downs = [rows], [rows]
    for _ in range(1, mid):
        ups.append([along_z(x, 1) for x in ups[-1]])
        downs.append([along_z(x, -1) for x in downs[-1]])
    far = [along_z(ups[-1][0], 1), along_z(downs[-1][1], -1)]
    held = {k: ups[k] for k in range(mid)} | {-k: downs[k] for k in range(1, mid)} | {mid: far}
    blocks = {k: [(x, j * half) for j, x in enumerate(held[k])] for k in held}

    rest_came = from_swapped(after(rest_gu, ups[1]))
    early_came = from_swapped(after(early_down, ups[2]))
    late_came = from_swapped(after(late_down, ups[3]))
    near_gu = pick(near_gu, after(near_came, ups[2]))
    near_other = other_core(near_gu)
    sums = gate_up([blocks[k] for k in near], [near_gu, near_other])
    rest_gu = pick(rest_gu, after(rest_came, ups[3], downs[3]))
    rest_other = other_core(rest_gu)
    hidden = gate_up([blocks[k] for k in rest], [rest_gu, rest_other], sums, last=True)

    early_down = pick(early_down, after(early_came, far))
    early_other = other_core(early_down)
    early_down = jnp.concatenate([early_down, early_other], axis=1)

    def share(w):
        return lax.optimization_barrier(jnp.dot(hidden, w, preferred_element_type=jnp.float32))

    def add(mine, j, came):
        return mine[j * half : (j + 1) * half] + came.astype(jnp.float32)

    first = share(early_down[rest.index(mid)])
    up = [along_z(first[:half].astype(jnp.bfloat16), 1), None]
    dn = [None, along_z(first[half:].astype(jnp.bfloat16), -1)]
    late_down = pick(late_down, after(late_came, up[0]))
    late_other = other_core(late_down)
    late_down = jnp.concatenate([late_down, late_other], axis=1)
    table = {k: early_down[j] for j, k in enumerate(rest)} | {k: late_down[j] for j, k in enumerate(near)}
    for k in range(mid - 1, 0, -1):
        for chain, step in ((up, 1), (dn, -1)):
            mine = share(table[k * step])
            for j in (0, 1) if step > 0 else (1, 0):
                sent = mine[j * half : (j + 1) * half] if chain[j] is None else add(mine, j, chain[j])
                chain[j] = along_z(sent.astype(jnp.bfloat16), step)
    mine = share(table[0])
    produced = jnp.concatenate([add(mine, j, up[j]) + dn[j].astype(jnp.float32) for j in (0, 1)], axis=0)
    produced = produced.astype(jnp.bfloat16)

    back = produced.reshape(owners, capacity, 2, width).transpose(0, 2, 1, 3)
    returned = lax.all_to_all(
        back.reshape(experts, capacity, width), PLANE, split_axis=0, concat_axis=0, tiled=True
    ).reshape(slot_count, width)
    mixed = jnp.zeros((rows_dev, width), jnp.float32)
    for k in range(TOP):
        result = jnp.dot(
            picks_k[k].astype(jnp.bfloat16), returned, preferred_element_type=jnp.float32
        )
        mixed = mixed + route_weight[:, k][:, None] * result
    return mixed.astype(jnp.bfloat16)


def solution(mesh):
    fine = Mesh(mesh.devices.reshape(SHAPE), NAMES)
    expert, hidden = ("xl", "y", "core"), ("z", "xh")
    in_specs = (
        P(expert, hidden),
        P(expert, None),
        P(expert, None),
        P(expert, None, hidden),
        P(expert, None, hidden),
        P(expert, hidden, None),
    )
    return jax.shard_map(
        on_device, mesh=fine, in_specs=in_specs, out_specs=P(expert, hidden), check_vma=False
    )
```

```python
import jax
import jax.numpy as jnp
from jax import lax
from jax.experimental import pallas as pl
from jax.experimental.pallas import tpu as pltpu
from jax.sharding import Mesh, PartitionSpec as P

TOP = 2
SHAPE = (2, 4, 2, 8, 2)
NAMES = ("xl", "y", "core", "z", "xh")
PLANE = ("xl", "y", "xh")


def along_z(x, step):
    n = lax.axis_size("z")
    return lax.ppermute(x, "z", [(s, (s + step) % n) for s in range(n)])


def from_swapped(x):
    return lax.ppermute(x, ("core", "xh"), [(1, 2), (2, 1)])


def after(x, *others):
    return lax.optimization_barrier((x, others))[0]


def other_core(x):
    return lax.ppermute(x, "core", [(0, 1), (1, 0)])


def add_blocks(tops, counts, units, held, weights, total):
    step = pl.program_id(0)
    taken = 0
    for k, count in enumerate(counts):
        parts = [(held[j], tops[j]) for j in range(taken, taken + count)]
        taken += count

        @pl.when(step == k)
        def _():
            w = jnp.concatenate([w_ref[...] for w_ref in weights], axis=1)
            for x_ref, top in parts:
                at = pl.ds(top, x_ref.shape[0])
                total[at, :] += jnp.dot(x_ref[...], w, preferred_element_type=jnp.float32)


def near_body(tops, counts, units, *refs):
    held, (own_ref, other_ref, *before, out_ref) = refs[: len(tops)], refs[len(tops) :]

    @pl.when(pl.program_id(0) == 0)
    def _():
        out_ref[...] = before[0][...] if before else jnp.zeros_like(out_ref)

    add_blocks(tops, counts, units, held, (own_ref, other_ref), out_ref)


def rest_body(tops, counts, units, n, at_ref, *refs):
    held, refs = refs[: len(tops)], refs[len(tops) :]
    own_ref, other_ref, before_ref = refs[:3]
    down_refs, refs = refs[3 : 3 + 2 * n], refs[3 + 2 * n :]
    hidden_ref, first_ref, share_refs, total = refs[0], refs[1], refs[2:-1], refs[-1]
    step = pl.program_id(0)

    @pl.when(step == 0)
    def _():
        total[...] = before_ref[...]

    add_blocks(tops, counts, units, held, (own_ref, other_ref), total)

    @pl.when(step == len(counts) - 1)
    def _():
        for j in range(2):
            gate = total[:, 2 * j * units : (2 * j + 1) * units]
            up = total[:, (2 * j + 1) * units : (2 * j + 2) * units]
            act = gate / (1.0 + jnp.exp(-gate)) * up
            hidden_ref[:, j * units : (j + 1) * units] = act.astype(jnp.bfloat16)
        hidden = hidden_ref[...]
        for j in range(n):
            w = jnp.concatenate([down_refs[2 * j][...], down_refs[2 * j + 1][...]], axis=0)
            out = jnp.dot(hidden, w, preferred_element_type=jnp.float32)
            if j == 0:
                first_ref[...] = out.astype(jnp.bfloat16)
            else:
                share_refs[j - 1][...] = out


WHOLE = pl.BlockSpec(memory_space=pltpu.VMEM)


def sizes(blocks, weights):
    held = [x for parts in blocks for x, _ in parts]
    tops = [top for parts in blocks for _, top in parts]
    counts = [len(parts) for parts in blocks]
    units = weights[0].shape[1] // 2
    w_spec = pl.BlockSpec((held[0].shape[1], 2 * units), lambda k: (k, 0))
    return held, tops, counts, units, w_spec


def gate_up_near(blocks, weights, before=()):
    held, tops, counts, units, w_spec = sizes(blocks, weights)
    rows, depth = held[0].shape
    out = (rows, 4 * units)
    return pl.pallas_call(
        lambda *refs: near_body(tops, counts, units, *refs),
        grid=(len(blocks),),
        in_specs=[WHOLE] * len(held) + [w_spec] * 2 + [WHOLE] * len(before),
        out_specs=pl.BlockSpec(out, lambda k: (0, 0)),
        out_shape=jax.ShapeDtypeStruct(out, jnp.float32),
        compiler_params=pltpu.CompilerParams(vmem_limit_bytes=24 << 20),
        cost_estimate=pl.CostEstimate(
            flops=8 * len(blocks) * rows * depth * units,
            bytes_accessed=2 * len(blocks) * depth * (rows + 4 * units),
            transcendentals=0,
        ),
    )(*held, *weights, *before)


def gate_up_rest(blocks, skipped, weights, before, at, n, down):
    held, tops, counts, units, w_spec = sizes(blocks, weights)
    rows, depth = before.shape[0], held[0].shape[1]
    w_spec = pl.BlockSpec(w_spec.block_shape, lambda k, at_ref: (k + skipped, 0))
    d_specs = [
        pl.BlockSpec((units, depth), lambda k, at_ref, j=j: (0, at_ref[j])) for j in range(n) for _ in down
    ]
    out_shape = [
        jax.ShapeDtypeStruct((rows, 2 * units), jnp.bfloat16),
        jax.ShapeDtypeStruct((rows, depth), jnp.bfloat16),
    ] + [jax.ShapeDtypeStruct((rows, depth), jnp.float32)] * (n - 1)
    return pl.pallas_call(
        lambda *refs: rest_body(tops, counts, units, n, *refs),
        grid_spec=pltpu.PrefetchScalarGridSpec(
            num_scalar_prefetch=1,
            grid=(len(blocks),),
            in_specs=[WHOLE] * len(held) + [w_spec] * 2 + [WHOLE] + d_specs,
            out_specs=[pl.BlockSpec(o.shape, lambda k, at_ref: (0, 0)) for o in out_shape],
            scratch_shapes=[pltpu.VMEM((rows, 4 * units), jnp.float32)],
        ),
        out_shape=out_shape,
        compiler_params=pltpu.CompilerParams(vmem_limit_bytes=32 << 20),
        cost_estimate=pl.CostEstimate(
            flops=8 * len(blocks) * rows * depth * units + 4 * n * rows * units * depth,
            bytes_accessed=2 * len(blocks) * depth * (rows + 4 * units) + 8 * n * units * depth,
            transcendentals=2 * rows * units,
        ),
    )(at, *held, *weights, before, *(list(down) * n))


def shares_body(at_ref, hidden_ref, own_ref, other_ref, *out_refs):
    w = jnp.concatenate([own_ref[...], other_ref[...]], axis=0)
    out = jnp.dot(hidden_ref[...], w, preferred_element_type=jnp.float32)
    for k, out_ref in enumerate(out_refs):

        @pl.when(pl.program_id(0) == k)
        def _():
            out_ref[...] = out


def shares(hidden, at, n, width, down):
    rows, units = hidden.shape[0], down[0].shape[0]
    last = at.shape[0] - n
    spec = pl.BlockSpec((units, width), lambda k, at_ref: (0, at_ref[k + n]))
    return pl.pallas_call(
        shares_body,
        grid_spec=pltpu.PrefetchScalarGridSpec(
            num_scalar_prefetch=1,
            grid=(last,),
            in_specs=[WHOLE, spec, spec],
            out_specs=[pl.BlockSpec((rows, width), lambda k, at_ref: (0, 0))] * last,
        ),
        out_shape=[jax.ShapeDtypeStruct((rows, width), jnp.float32)] * last,
        compiler_params=pltpu.CompilerParams(vmem_limit_bytes=32 << 20),
        cost_estimate=pl.CostEstimate(
            flops=4 * last * rows * units * width,
            bytes_accessed=4 * last * (units + rows) * width,
            transcendentals=0,
        ),
    )(at, hidden, *down)


def pack_gate_up_body(units, at_ref, gate_ref, up_ref, out_ref):
    out_ref[:, :units] = gate_ref[...]
    out_ref[:, units:] = up_ref[...]


def pack_gate_up(at, gate, up, depth):
    n, units = at.shape[0], gate.shape[1]
    spec = pl.BlockSpec((depth, units), lambda k, at_ref: (at_ref[k], 0))
    return pl.pallas_call(
        lambda *refs: pack_gate_up_body(units, *refs),
        grid_spec=pltpu.PrefetchScalarGridSpec(
            num_scalar_prefetch=1,
            grid=(n,),
            in_specs=[spec, spec],
            out_specs=pl.BlockSpec((depth, 2 * units), lambda k, at_ref: (k, 0)),
        ),
        out_shape=jax.ShapeDtypeStruct((n * depth, 2 * units), jnp.bfloat16),
        cost_estimate=pl.CostEstimate(
            flops=0, bytes_accessed=8 * n * depth * units, transcendentals=0
        ),
    )(at, gate, up)


def on_device(tokens, route_ids, route_weight, w_gate, w_up, w_down):
    rows_dev, width = tokens.shape
    experts = lax.axis_size(PLANE)
    nz = lax.axis_size("z")
    z = lax.axis_index("z")
    capacity = (rows_dev * TOP * 5 + 4 * experts - 1) // (4 * experts)
    slot_count = experts * capacity
    owners = experts // 2
    units = w_gate.shape[2]

    matches = route_ids[:, :, None] == jnp.arange(experts, dtype=jnp.int32)[None, None, :]
    chosen = jnp.any(matches, axis=1)
    before = jnp.arange(rows_dev)[:, None] > jnp.arange(rows_dev)[None, :]
    ranking = jnp.dot(
        before.astype(jnp.bfloat16), chosen.astype(jnp.bfloat16), preferred_element_type=jnp.float32
    )
    slot_of = jnp.arange(experts, dtype=jnp.float32)[None, :] * capacity + ranking
    slot_k = jnp.sum(jnp.where(matches, slot_of[:, None, :], 0.0), axis=2).astype(jnp.int32)
    slots = jnp.arange(slot_count, dtype=jnp.int32)
    picks_k = [slot_k[:, k][:, None] == slots[None, :] for k in range(TOP)]
    picks = (picks_k[0] | picks_k[1]).astype(jnp.bfloat16)

    leaving = lax.dot_general(
        picks, tokens, (((0,), (0,)), ((), ())), preferred_element_type=jnp.float32
    ).astype(jnp.bfloat16)
    arrived = lax.all_to_all(
        leaving.reshape(experts, capacity, width), PLANE, split_axis=0, concat_axis=0, tiled=True
    )
    def at(places):
        return jnp.stack([(z + k) % nz for k in places]).astype(jnp.int32)

    def pick(mine, came):
        return jnp.where(lax.axis_index("core") == lax.axis_index("xh"), mine, came)

    mid = nz // 2
    near = [0, 1, -1]
    rest = [k for n in range(2, mid) for k in (n, -n)] + [mid]
    early = [mid, mid - 1, 1 - mid]
    late = [k for n in range(mid - 2, 0, -1) for k in (n, -n)] + [0]
    near_gu = pack_gate_up(at([-k for k in near]), w_gate[0], w_up[0], 2 * width)
    rest_gu = pack_gate_up(at([-k for k in rest]), w_gate[0], w_up[0], 2 * width)
    arrived, near_gu, rest_gu = lax.optimization_barrier((arrived, near_gu, rest_gu))
    near_came = from_swapped(near_gu)

    rows = arrived.reshape(owners, 2, capacity, width).transpose(0, 2, 1, 3)
    rows = rows.reshape(owners * capacity, 2 * width)
    half = owners * capacity // 2
    up1, down1 = along_z(rows, 1), along_z(rows, -1)

    rest_came = from_swapped(rest_gu)
    near_gu = pick(near_gu, near_came)
    up1, down1, near_gu = lax.optimization_barrier((up1, down1, near_gu))
    down_came = from_swapped(after(w_down[0], up1))
    up2, down2 = along_z(up1, 1), along_z(down1, -1)
    near_other = other_core(near_gu)
    block = {0: [(rows, 0)], 1: [(up1, 0)], -1: [(down1, 0)]}
    sums = gate_up_near([block[k] for k in near], [near_gu, near_other])

    up2, down2, sums = lax.optimization_barrier((up2, down2, sums))
    up3, down3 = along_z(up2, 1), along_z(down2, -1)
    rest_gu = pick(rest_gu, rest_came)
    own_down = pick(w_down[0], down_came)

    up3, down3, rest_gu, own_down = lax.optimization_barrier((up3, down3, rest_gu, own_down))
    far = [along_z(up3[:half], 1), along_z(down3[half:], -1)]
    rest_other = other_core(rest_gu)
    down_w = [own_down, other_core(own_down)]
    block |= {2: [(up2, 0)], -2: [(down2, 0)], 3: [(up3, 0)], -3: [(down3, 0)]}
    block[mid] = [(far[0], 0), (far[1], half)]
    to = at(early + late)
    rest_w = [rest_gu, rest_other]
    sums = gate_up_near([block[k] for k in rest[:-1]], rest_w, [sums])
    hidden, first, *early_sums = gate_up_rest(
        [block[mid]], len(rest) - 1, rest_w, sums, to, len(early), down_w
    )

    up, dn = along_z(first[:half], 1), along_z(first[half:], -1)
    late_sums = shares(hidden, to, len(early), 2 * width, down_w)
    table = {k: early_sums[j - 1] for j, k in enumerate(early)} | {k: late_sums[j] for j, k in enumerate(late)}
    for k in range(mid - 1, 0, -1):
        mine, theirs = table[k], table[-k]
        if k == mid - 1:
            mine = jnp.concatenate([mine[:half] + up.astype(jnp.float32), mine[half:]], axis=0)
            theirs = jnp.concatenate([theirs[:half], theirs[half:] + dn.astype(jnp.float32)], axis=0)
        else:
            mine, theirs = mine + up.astype(jnp.float32), theirs + dn.astype(jnp.float32)
        up = along_z(mine.astype(jnp.bfloat16), 1)
        dn = along_z(theirs.astype(jnp.bfloat16), -1)
    produced = table[0] + up.astype(jnp.float32) + dn.astype(jnp.float32)
    produced = produced.astype(jnp.bfloat16)

    back = produced.reshape(owners, capacity, 2, width).transpose(0, 2, 1, 3)
    returned = lax.all_to_all(
        back.reshape(experts, capacity, width), PLANE, split_axis=0, concat_axis=0, tiled=True
    ).reshape(slot_count, width)
    mixed = jnp.zeros((rows_dev, width), jnp.float32)
    for k in range(TOP):
        result = jnp.dot(
            picks_k[k].astype(jnp.bfloat16), returned, preferred_element_type=jnp.float32
        )
        mixed = mixed + route_weight[:, k][:, None] * result
    return mixed.astype(jnp.bfloat16)


def solution(mesh):
    fine = Mesh(mesh.devices.reshape(SHAPE), NAMES)
    expert, hidden = ("xl", "y", "core"), ("z", "xh")
    in_specs = (
        P(expert, hidden),
        P(expert, None),
        P(expert, None),
        P(expert, None, hidden),
        P(expert, None, hidden),
        P(expert, hidden, None),
    )
    return jax.shard_map(
        on_device, mesh=fine, in_specs=in_specs, out_specs=P(expert, hidden), check_vma=False
    )
```

```python
import jax
import jax.numpy as jnp
from jax import lax
from jax.experimental import pallas as pl
from jax.experimental.pallas import tpu as pltpu
from jax.sharding import Mesh, PartitionSpec as P

TOP = 2
SHAPE = (2, 4, 2, 8, 2)
NAMES = ("xl", "y", "core", "z", "xh")
PLANE = ("xl", "y", "xh")


def along_z(x, step):
    n = lax.axis_size("z")
    return lax.ppermute(x, "z", [(s, (s + step) % n) for s in range(n)])


def from_swapped(x):
    return lax.ppermute(x, ("core", "xh"), [(1, 2), (2, 1)])


def after(x, *others):
    return lax.optimization_barrier((x, others))[0]


def other_core(x):
    return lax.ppermute(x, "core", [(0, 1), (1, 0)])


def add_blocks(tops, counts, units, held, weights, total):
    step = pl.program_id(0)
    taken = 0
    for k, count in enumerate(counts):
        parts = [(held[j], tops[j]) for j in range(taken, taken + count)]
        taken += count

        @pl.when(step == k)
        def _():
            w = jnp.concatenate([w_ref[...] for w_ref in weights], axis=1)
            for x_ref, top in parts:
                at = pl.ds(top, x_ref.shape[0])
                total[at, :] += jnp.dot(x_ref[...], w, preferred_element_type=jnp.float32)


def near_body(tops, counts, units, *refs):
    held, (own_ref, other_ref, *before, out_ref) = refs[: len(tops)], refs[len(tops) :]

    @pl.when(pl.program_id(0) == 0)
    def _():
        out_ref[...] = before[0][...] if before else jnp.zeros_like(out_ref)

    add_blocks(tops, counts, units, held, (own_ref, other_ref), out_ref)


def rest_body(tops, counts, units, n, at_ref, *refs):
    held, refs = refs[: len(tops)], refs[len(tops) :]
    own_ref, other_ref, before_ref = refs[:3]
    down_refs, refs = refs[3 : 3 + 2 * n], refs[3 + 2 * n :]
    hidden_ref, out_refs, total = refs[0], refs[1:-1], refs[-1]
    step = pl.program_id(0)

    @pl.when(step == 0)
    def _():
        total[...] = before_ref[...]

    add_blocks(tops, counts, units, held, (own_ref, other_ref), total)

    @pl.when(step == len(counts) - 1)
    def _():
        for j in range(2):
            gate = total[:, 2 * j * units : (2 * j + 1) * units]
            up = total[:, (2 * j + 1) * units : (2 * j + 2) * units]
            act = gate / (1.0 + jnp.exp(-gate)) * up
            hidden_ref[:, j * units : (j + 1) * units] = act.astype(jnp.bfloat16)
        hidden = hidden_ref[...]
        for j in range(n):
            w = jnp.concatenate([down_refs[2 * j][...], down_refs[2 * j + 1][...]], axis=0)
            out = jnp.dot(hidden, w, preferred_element_type=jnp.float32)
            put_halves(out, out_refs[2 * j : 2 * j + 2])


def put_halves(out, refs):
    half = refs[0].shape[0]
    for j, ref in enumerate(refs):
        ref[...] = out[j * half : (j + 1) * half].astype(ref.dtype)


WHOLE = pl.BlockSpec(memory_space=pltpu.VMEM)


def sizes(blocks, weights):
    held = [x for parts in blocks for x, _ in parts]
    tops = [top for parts in blocks for _, top in parts]
    counts = [len(parts) for parts in blocks]
    units = weights[0].shape[1] // 2
    w_spec = pl.BlockSpec((held[0].shape[1], 2 * units), lambda k: (k, 0))
    return held, tops, counts, units, w_spec


def gate_up_near(blocks, weights, before=()):
    held, tops, counts, units, w_spec = sizes(blocks, weights)
    rows, depth = held[0].shape
    out = (rows, 4 * units)
    return pl.pallas_call(
        lambda *refs: near_body(tops, counts, units, *refs),
        grid=(len(blocks),),
        in_specs=[WHOLE] * len(held) + [w_spec] * 2 + [WHOLE] * len(before),
        out_specs=pl.BlockSpec(out, lambda k: (0, 0)),
        out_shape=jax.ShapeDtypeStruct(out, jnp.float32),
        compiler_params=pltpu.CompilerParams(vmem_limit_bytes=24 << 20),
        cost_estimate=pl.CostEstimate(
            flops=8 * len(blocks) * rows * depth * units,
            bytes_accessed=2 * len(blocks) * depth * (rows + 4 * units),
            transcendentals=0,
        ),
    )(*held, *weights, *before)


def gate_up_rest(blocks, skipped, weights, before, at, types, down):
    n = len(types)
    held, tops, counts, units, w_spec = sizes(blocks, weights)
    rows, depth = before.shape[0], held[0].shape[1]
    w_spec = pl.BlockSpec(w_spec.block_shape, lambda k, at_ref: (k + skipped, 0))
    d_specs = [
        pl.BlockSpec((units, depth), lambda k, at_ref, j=j: (0, at_ref[j])) for j in range(n) for _ in down
    ]
    out_shape = [jax.ShapeDtypeStruct((rows, 2 * units), jnp.bfloat16)]
    out_shape += [jax.ShapeDtypeStruct((rows // 2, depth), t) for pair in types for t in pair]
    return pl.pallas_call(
        lambda *refs: rest_body(tops, counts, units, n, *refs),
        grid_spec=pltpu.PrefetchScalarGridSpec(
            num_scalar_prefetch=1,
            grid=(len(blocks),),
            in_specs=[WHOLE] * len(held) + [w_spec] * 2 + [WHOLE] + d_specs,
            out_specs=[pl.BlockSpec(o.shape, lambda k, at_ref: (0, 0)) for o in out_shape],
            scratch_shapes=[pltpu.VMEM((rows, 4 * units), jnp.float32)],
        ),
        out_shape=out_shape,
        compiler_params=pltpu.CompilerParams(vmem_limit_bytes=32 << 20),
        cost_estimate=pl.CostEstimate(
            flops=8 * len(blocks) * rows * depth * units + 4 * n * rows * units * depth,
            bytes_accessed=2 * len(blocks) * depth * (rows + 4 * units) + 8 * n * units * depth,
            transcendentals=2 * rows * units,
        ),
    )(at, *held, *weights, before, *(list(down) * n))


def shares_body(at_ref, hidden_ref, own_ref, other_ref, *out_refs):
    w = jnp.concatenate([own_ref[...], other_ref[...]], axis=0)
    out = jnp.dot(hidden_ref[...], w, preferred_element_type=jnp.float32)
    for k in range(len(out_refs) // 2):

        @pl.when(pl.program_id(0) == k)
        def _():
            put_halves(out, out_refs[2 * k : 2 * k + 2])


def shares(hidden, at, n, width, down):
    rows, units = hidden.shape[0], down[0].shape[0]
    last = at.shape[0] - n
    spec = pl.BlockSpec((units, width), lambda k, at_ref: (0, at_ref[k + n]))
    return pl.pallas_call(
        shares_body,
        grid_spec=pltpu.PrefetchScalarGridSpec(
            num_scalar_prefetch=1,
            grid=(last,),
            in_specs=[WHOLE, spec, spec],
            out_specs=[pl.BlockSpec((rows // 2, width), lambda k, at_ref: (0, 0))] * (2 * last),
        ),
        out_shape=[jax.ShapeDtypeStruct((rows // 2, width), jnp.float32)] * (2 * last),
        compiler_params=pltpu.CompilerParams(vmem_limit_bytes=32 << 20),
        cost_estimate=pl.CostEstimate(
            flops=4 * last * rows * units * width,
            bytes_accessed=4 * last * (units + rows) * width,
            transcendentals=0,
        ),
    )(at, hidden, *down)


def pack_gate_up_body(units, at_ref, gate_ref, up_ref, out_ref):
    out_ref[:, :units] = gate_ref[...]
    out_ref[:, units:] = up_ref[...]


def pack_gate_up(at, gate, up, depth):
    n, units = at.shape[0], gate.shape[1]
    spec = pl.BlockSpec((depth, units), lambda k, at_ref: (at_ref[k], 0))
    return pl.pallas_call(
        lambda *refs: pack_gate_up_body(units, *refs),
        grid_spec=pltpu.PrefetchScalarGridSpec(
            num_scalar_prefetch=1,
            grid=(n,),
            in_specs=[spec, spec],
            out_specs=pl.BlockSpec((depth, 2 * units), lambda k, at_ref: (k, 0)),
        ),
        out_shape=jax.ShapeDtypeStruct((n * depth, 2 * units), jnp.bfloat16),
        cost_estimate=pl.CostEstimate(
            flops=0, bytes_accessed=8 * n * depth * units, transcendentals=0
        ),
    )(at, gate, up)


def on_device(tokens, route_ids, route_weight, w_gate, w_up, w_down):
    rows_dev, width = tokens.shape
    experts = lax.axis_size(PLANE)
    nz = lax.axis_size("z")
    z = lax.axis_index("z")
    capacity = (rows_dev * TOP * 5 + 4 * experts - 1) // (4 * experts)
    slot_count = experts * capacity
    owners = experts // 2
    units = w_gate.shape[2]

    matches = route_ids[:, :, None] == jnp.arange(experts, dtype=jnp.int32)[None, None, :]
    chosen = jnp.any(matches, axis=1)
    before = jnp.arange(rows_dev)[:, None] > jnp.arange(rows_dev)[None, :]
    ranking = jnp.dot(
        before.astype(jnp.bfloat16), chosen.astype(jnp.bfloat16), preferred_element_type=jnp.float32
    )
    slot_of = jnp.arange(experts, dtype=jnp.float32)[None, :] * capacity + ranking
    slot_k = jnp.sum(jnp.where(matches, slot_of[:, None, :], 0.0), axis=2).astype(jnp.int32)
    slots = jnp.arange(slot_count, dtype=jnp.int32)
    picks_k = [slot_k[:, k][:, None] == slots[None, :] for k in range(TOP)]
    picks = (picks_k[0] | picks_k[1]).astype(jnp.bfloat16)

    leaving = lax.dot_general(
        picks, tokens, (((0,), (0,)), ((), ())), preferred_element_type=jnp.float32
    ).astype(jnp.bfloat16)
    arrived = lax.all_to_all(
        leaving.reshape(experts, capacity, width), PLANE, split_axis=0, concat_axis=0, tiled=True
    )
    def at(places):
        return jnp.stack([(z + k) % nz for k in places]).astype(jnp.int32)

    def pick(mine, came):
        return jnp.where(lax.axis_index("core") == lax.axis_index("xh"), mine, came)

    mid = nz // 2
    near = [0, 1, -1]
    rest = [k for n in range(2, mid) for k in (n, -n)] + [mid]
    early = [mid, mid - 1, 1 - mid]
    late = [k for n in range(mid - 2, 0, -1) for k in (n, -n)] + [0]
    near_gu = pack_gate_up(at([-k for k in near]), w_gate[0], w_up[0], 2 * width)
    rest_gu = pack_gate_up(at([-k for k in rest]), w_gate[0], w_up[0], 2 * width)
    arrived, near_gu, rest_gu = lax.optimization_barrier((arrived, near_gu, rest_gu))
    near_came = from_swapped(near_gu)

    rows = arrived.reshape(owners, 2, capacity, width).transpose(0, 2, 1, 3)
    rows = rows.reshape(owners * capacity, 2 * width)
    half = owners * capacity // 2
    up1, down1 = along_z(rows, 1), along_z(rows, -1)

    rest_came = from_swapped(rest_gu)
    near_gu = pick(near_gu, near_came)
    up1, down1, near_gu = lax.optimization_barrier((up1, down1, near_gu))
    down_came = from_swapped(after(w_down[0], up1))
    up2, down2 = along_z(up1, 1), along_z(down1, -1)
    near_other = other_core(near_gu)
    block = {0: [(rows, 0)], 1: [(up1, 0)], -1: [(down1, 0)]}
    sums = gate_up_near([block[k] for k in near], [near_gu, near_other])

    up2, down2, sums = lax.optimization_barrier((up2, down2, sums))
    up3, down3 = along_z(up2, 1), along_z(down2, -1)
    rest_gu = pick(rest_gu, rest_came)
    own_down = pick(w_down[0], down_came)

    up3, down3, rest_gu = lax.optimization_barrier((up3, down3, rest_gu))
    far = [along_z(up3[:half], 1), along_z(down3[half:], -1)]
    rest_other = other_core(rest_gu)
    down_w = [own_down, other_core(own_down)]
    block |= {2: [(up2, 0)], -2: [(down2, 0)], 3: [(up3, 0)], -3: [(down3, 0)]}
    block[mid] = [(far[0], 0), (far[1], half)]
    to = at(early + late)
    rest_w = [rest_gu, rest_other]
    sums = gate_up_near([block[k] for k in rest[:-1]], rest_w, [sums])
    wide, short = jnp.float32, jnp.bfloat16
    hidden, *sums = gate_up_rest(
        [block[mid]], len(rest) - 1, rest_w, sums, to, [(short, short), (wide, short), (short, wide)], down_w
    )

    def add(mine, came):
        return (mine + came.astype(jnp.float32)).astype(jnp.bfloat16)

    ups = [along_z(sums[0], 1), along_z(sums[3], 1)]
    downs = [along_z(sums[4], -1), along_z(sums[1], -1)]
    late_sums = shares(hidden, to, len(early), 2 * width, down_w)
    table = {k: late_sums[2 * j : 2 * j + 2] for j, k in enumerate(late)}
    ups[0] = along_z(add(sums[2], ups[0]), 1)
    downs[1] = along_z(add(sums[5], downs[1]), -1)
    for k in range(mid - 2, 0, -1):
        for j in (0, 1):
            ups[1 - j] = along_z(add(table[k][1 - j], ups[1 - j]), 1)
            downs[j] = along_z(add(table[-k][j], downs[j]), -1)
    produced = jnp.concatenate(
        [add(mine + up.astype(jnp.float32), dn) for mine, up, dn in zip(table[0], ups, downs)], axis=0
    )

    back = produced.reshape(owners, capacity, 2, width).transpose(0, 2, 1, 3)
    returned = lax.all_to_all(
        back.reshape(experts, capacity, width), PLANE, split_axis=0, concat_axis=0, tiled=True
    ).reshape(slot_count, width)
    mixed = jnp.zeros((rows_dev, width), jnp.float32)
    for k in range(TOP):
        result = jnp.dot(
            picks_k[k].astype(jnp.bfloat16), returned, preferred_element_type=jnp.float32
        )
        mixed = mixed + route_weight[:, k][:, None] * result
    return mixed.astype(jnp.bfloat16)


def solution(mesh):
    fine = Mesh(mesh.devices.reshape(SHAPE), NAMES)
    expert, hidden = ("xl", "y", "core"), ("z", "xh")
    in_specs = (
        P(expert, hidden),
        P(expert, None),
        P(expert, None),
        P(expert, None, hidden),
        P(expert, None, hidden),
        P(expert, hidden, None),
    )
    return jax.shard_map(
        on_device, mesh=fine, in_specs=in_specs, out_specs=P(expert, hidden), check_vma=False
    )
```

```python
import jax
import jax.numpy as jnp
from jax import lax
from jax.experimental import pallas as pl
from jax.experimental.pallas import tpu as pltpu
from jax.sharding import Mesh, PartitionSpec as P

TOP = 2
SHAPE = (2, 4, 2, 8, 2)
NAMES = ("xl", "y", "core", "z", "xh")
PLANE = ("xl", "y", "xh")


def along_z(x, step):
    n = lax.axis_size("z")
    return lax.ppermute(x, "z", [(s, (s + step) % n) for s in range(n)])


def from_swapped(x):
    return lax.ppermute(x, ("core", "xh"), [(1, 2), (2, 1)])


def after(x, *others):
    return lax.optimization_barrier((x, others))[0]


def other_core(x):
    return lax.ppermute(x, "core", [(0, 1), (1, 0)])


def add_blocks(tops, counts, units, held, weights, total):
    step = pl.program_id(0)
    taken = 0
    for k, count in enumerate(counts):
        parts = [(held[j], tops[j]) for j in range(taken, taken + count)]
        taken += count

        @pl.when(step == k)
        def _():
            w = jnp.concatenate([w_ref[...] for w_ref in weights], axis=1)
            for x_ref, top in parts:
                at = pl.ds(top, x_ref.shape[0])
                total[at, :] += jnp.dot(x_ref[...], w, preferred_element_type=jnp.float32)


def near_body(tops, counts, units, *refs):
    held, (own_ref, other_ref, *before, out_ref) = refs[: len(tops)], refs[len(tops) :]

    @pl.when(pl.program_id(0) == 0)
    def _():
        out_ref[...] = before[0][...] if before else jnp.zeros_like(out_ref)

    add_blocks(tops, counts, units, held, (own_ref, other_ref), out_ref)


def rest_body(tops, counts, units, n, at_ref, *refs):
    held, refs = refs[: len(tops)], refs[len(tops) :]
    own_ref, other_ref, before_ref = refs[:3]
    down_refs, refs = refs[3 : 3 + 2 * n], refs[3 + 2 * n :]
    hidden_ref, out_refs, total = refs[0], refs[1:-1], refs[-1]
    step = pl.program_id(0)

    @pl.when(step == 0)
    def _():
        total[...] = before_ref[...]

    add_blocks(tops, counts, units, held, (own_ref, other_ref), total)

    @pl.when(step == len(counts) - 1)
    def _():
        for j in range(2):
            gate = total[:, 2 * j * units : (2 * j + 1) * units]
            up = total[:, (2 * j + 1) * units : (2 * j + 2) * units]
            act = gate / (1.0 + jnp.exp(-gate)) * up
            hidden_ref[:, j * units : (j + 1) * units] = act.astype(jnp.bfloat16)
        hidden = hidden_ref[...]
        for j in range(n):
            w = jnp.concatenate([down_refs[2 * j][...], down_refs[2 * j + 1][...]], axis=0)
            out = jnp.dot(hidden, w, preferred_element_type=jnp.float32)
            put_halves(out, out_refs[2 * j : 2 * j + 2])


def put_halves(out, refs):
    half = refs[0].shape[0]
    for j, ref in enumerate(refs):
        ref[...] = out[j * half : (j + 1) * half].astype(ref.dtype)


WHOLE = pl.BlockSpec(memory_space=pltpu.VMEM)


def sizes(blocks, weights):
    held = [x for parts in blocks for x, _ in parts]
    tops = [top for parts in blocks for _, top in parts]
    counts = [len(parts) for parts in blocks]
    units = weights[0].shape[1] // 2
    w_spec = pl.BlockSpec((held[0].shape[1], 2 * units), lambda k: (k, 0))
    return held, tops, counts, units, w_spec


def gate_up_near(blocks, weights, before=()):
    held, tops, counts, units, w_spec = sizes(blocks, weights)
    rows, depth = held[0].shape
    out = (rows, 4 * units)
    return pl.pallas_call(
        lambda *refs: near_body(tops, counts, units, *refs),
        grid=(len(blocks),),
        in_specs=[WHOLE] * len(held) + [w_spec] * 2 + [WHOLE] * len(before),
        out_specs=pl.BlockSpec(out, lambda k: (0, 0)),
        out_shape=jax.ShapeDtypeStruct(out, jnp.float32),
        compiler_params=pltpu.CompilerParams(vmem_limit_bytes=24 << 20),
        cost_estimate=pl.CostEstimate(
            flops=8 * len(blocks) * rows * depth * units,
            bytes_accessed=2 * len(blocks) * depth * (rows + 4 * units),
            transcendentals=0,
        ),
    )(*held, *weights, *before)


def gate_up_rest(blocks, skipped, weights, before, at, types, down):
    n = len(types)
    held, tops, counts, units, w_spec = sizes(blocks, weights)
    rows, depth = before.shape[0], held[0].shape[1]
    w_spec = pl.BlockSpec(w_spec.block_shape, lambda k, at_ref: (k + skipped, 0))
    d_specs = [
        pl.BlockSpec((units, depth), lambda k, at_ref, j=j: (0, at_ref[j])) for j in range(n) for _ in down
    ]
    out_shape = [jax.ShapeDtypeStruct((rows, 2 * units), jnp.bfloat16)]
    out_shape += [jax.ShapeDtypeStruct((rows // 2, depth), t) for pair in types for t in pair]
    return pl.pallas_call(
        lambda *refs: rest_body(tops, counts, units, n, *refs),
        grid_spec=pltpu.PrefetchScalarGridSpec(
            num_scalar_prefetch=1,
            grid=(len(blocks),),
            in_specs=[WHOLE] * len(held) + [w_spec] * 2 + [WHOLE] + d_specs,
            out_specs=[pl.BlockSpec(o.shape, lambda k, at_ref: (0, 0)) for o in out_shape],
            scratch_shapes=[pltpu.VMEM((rows, 4 * units), jnp.float32)],
        ),
        out_shape=out_shape,
        compiler_params=pltpu.CompilerParams(vmem_limit_bytes=32 << 20),
        cost_estimate=pl.CostEstimate(
            flops=8 * len(blocks) * rows * depth * units + 4 * n * rows * units * depth,
            bytes_accessed=2 * len(blocks) * depth * (rows + 4 * units) + 8 * n * units * depth,
            transcendentals=2 * rows * units,
        ),
    )(at, *held, *weights, before, *(list(down) * n))


def shares_body(at_ref, hidden_ref, own_ref, other_ref, *out_refs):
    w = jnp.concatenate([own_ref[...], other_ref[...]], axis=0)
    out = jnp.dot(hidden_ref[...], w, preferred_element_type=jnp.float32)
    for k in range(len(out_refs) // 2):

        @pl.when(pl.program_id(0) == k)
        def _():
            put_halves(out, out_refs[2 * k : 2 * k + 2])


def shares(hidden, at, n, width, down):
    rows, units = hidden.shape[0], down[0].shape[0]
    last = at.shape[0] - n
    spec = pl.BlockSpec((units, width), lambda k, at_ref: (0, at_ref[k + n]))
    return pl.pallas_call(
        shares_body,
        grid_spec=pltpu.PrefetchScalarGridSpec(
            num_scalar_prefetch=1,
            grid=(last,),
            in_specs=[WHOLE, spec, spec],
            out_specs=[pl.BlockSpec((rows // 2, width), lambda k, at_ref: (0, 0))] * (2 * last),
        ),
        out_shape=[jax.ShapeDtypeStruct((rows // 2, width), jnp.float32)] * (2 * last),
        compiler_params=pltpu.CompilerParams(vmem_limit_bytes=32 << 20),
        cost_estimate=pl.CostEstimate(
            flops=4 * last * rows * units * width,
            bytes_accessed=4 * last * (units + rows) * width,
            transcendentals=0,
        ),
    )(at, hidden, *down)


def pack_gate_up_body(units, at_ref, gate_ref, up_ref, out_ref):
    out_ref[:, :units] = gate_ref[...]
    out_ref[:, units:] = up_ref[...]


def pack_gate_up(at, gate, up, depth):
    n, units = at.shape[0], gate.shape[1]
    spec = pl.BlockSpec((depth, units), lambda k, at_ref: (at_ref[k], 0))
    return pl.pallas_call(
        lambda *refs: pack_gate_up_body(units, *refs),
        grid_spec=pltpu.PrefetchScalarGridSpec(
            num_scalar_prefetch=1,
            grid=(n,),
            in_specs=[spec, spec],
            out_specs=pl.BlockSpec((depth, 2 * units), lambda k, at_ref: (k, 0)),
        ),
        out_shape=jax.ShapeDtypeStruct((n * depth, 2 * units), jnp.bfloat16),
        cost_estimate=pl.CostEstimate(
            flops=0, bytes_accessed=8 * n * depth * units, transcendentals=0
        ),
    )(at, gate, up)


def on_device(tokens, route_ids, route_weight, w_gate, w_up, w_down):
    rows_dev, width = tokens.shape
    experts = lax.axis_size(PLANE)
    nz = lax.axis_size("z")
    z = lax.axis_index("z")
    capacity = (rows_dev * TOP * 5 + 4 * experts - 1) // (4 * experts)
    slot_count = experts * capacity
    owners = experts // 2
    units = w_gate.shape[2]

    matches = route_ids[:, :, None] == jnp.arange(experts, dtype=jnp.int32)[None, None, :]
    chosen = jnp.any(matches, axis=1)
    before = jnp.arange(rows_dev)[:, None] > jnp.arange(rows_dev)[None, :]
    ranking = jnp.dot(
        before.astype(jnp.bfloat16), chosen.astype(jnp.bfloat16), preferred_element_type=jnp.float32
    )
    slot_of = jnp.arange(experts, dtype=jnp.float32)[None, :] * capacity + ranking
    slot_k = jnp.sum(jnp.where(matches, slot_of[:, None, :], 0.0), axis=2).astype(jnp.int32)
    slots = jnp.arange(slot_count, dtype=jnp.int32)
    picks_k = [slot_k[:, k][:, None] == slots[None, :] for k in range(TOP)]
    picks = (picks_k[0] | picks_k[1]).astype(jnp.bfloat16)

    leaving = lax.dot_general(
        picks, tokens, (((0,), (0,)), ((), ())), preferred_element_type=jnp.float32
    ).astype(jnp.bfloat16)
    arrived = lax.all_to_all(
        leaving.reshape(experts, capacity, width), PLANE, split_axis=0, concat_axis=0, tiled=True
    )
    def at(places):
        return jnp.stack([(z + k) % nz for k in places]).astype(jnp.int32)

    def pick(mine, came):
        return jnp.where(lax.axis_index("core") == lax.axis_index("xh"), mine, came)

    mid = nz // 2
    near = [0, 1, -1]
    rest = [k for n in range(2, mid) for k in (n, -n)] + [mid]
    early = [mid, mid - 1, 1 - mid]
    late = [k for n in range(mid - 2, 0, -1) for k in (n, -n)] + [0]
    near_gu = pack_gate_up(at([-k for k in near]), w_gate[0], w_up[0], 2 * width)
    rest_gu = pack_gate_up(at([-k for k in rest]), w_gate[0], w_up[0], 2 * width)
    part = units // 2
    down_came = [from_swapped(w_down[0, :part])]
    arrived, near_gu, rest_gu, down_came[0] = lax.optimization_barrier(
        (arrived, near_gu, rest_gu, down_came[0])
    )
    near_came = from_swapped(near_gu)

    rows = arrived.reshape(owners, 2, capacity, width).transpose(0, 2, 1, 3)
    rows = rows.reshape(owners * capacity, 2 * width)
    half = owners * capacity // 2
    up1, down1 = along_z(rows, 1), along_z(rows, -1)

    rest_came = from_swapped(after(rest_gu, rows))
    near_gu = pick(near_gu, near_came)
    up1, down1, near_gu = lax.optimization_barrier((up1, down1, near_gu))
    down_came.append(from_swapped(after(w_down[0], up1)[part:]))
    up2, down2 = along_z(up1, 1), along_z(down1, -1)
    near_other = other_core(near_gu)
    block = {0: [(rows, 0)], 1: [(up1, 0)], -1: [(down1, 0)]}
    sums = gate_up_near([block[k] for k in near], [near_gu, near_other])

    up2, down2, sums = lax.optimization_barrier((up2, down2, sums))
    up3, down3 = along_z(up2, 1), along_z(down2, -1)
    rest_gu = pick(rest_gu, rest_came)
    down_came = after(down_came, up2, down2)
    own_down = pick(w_down[0], jnp.concatenate(down_came, axis=0))

    up3, down3, rest_gu = lax.optimization_barrier((up3, down3, rest_gu))
    far = [along_z(up3[:half], 1), along_z(down3[half:], -1)]
    rest_other = other_core(rest_gu)
    down_w = [own_down, other_core(own_down)]
    block |= {2: [(up2, 0)], -2: [(down2, 0)], 3: [(up3, 0)], -3: [(down3, 0)]}
    block[mid] = [(far[0], 0), (far[1], half)]
    to = at(early + late)
    rest_w = [rest_gu, rest_other]
    sums = gate_up_near([block[k] for k in rest[:-1]], rest_w, [sums])
    wide, short = jnp.float32, jnp.bfloat16
    hidden, *sums = gate_up_rest(
        [block[mid]], len(rest) - 1, rest_w, sums, to, [(short, short), (wide, short), (short, wide)], down_w
    )

    def add(mine, came):
        return (mine + came.astype(jnp.float32)).astype(jnp.bfloat16)

    ups = [along_z(sums[0], 1), along_z(sums[3], 1)]
    downs = [along_z(sums[4], -1), along_z(sums[1], -1)]
    late_sums = shares(hidden, to, len(early), 2 * width, down_w)
    table = {k: late_sums[2 * j : 2 * j + 2] for j, k in enumerate(late)}
    ups[0] = along_z(add(sums[2], ups[0]), 1)
    downs[1] = along_z(add(sums[5], downs[1]), -1)
    for k in range(mid - 2, 0, -1):
        for j in (0, 1):
            ups[1 - j] = along_z(add(table[k][1 - j], ups[1 - j]), 1)
            downs[j] = along_z(add(table[-k][j], downs[j]), -1)
    produced = jnp.concatenate(
        [add(mine + up.astype(jnp.float32), dn) for mine, up, dn in zip(table[0], ups, downs)], axis=0
    )

    back = produced.reshape(owners, capacity, 2, width).transpose(0, 2, 1, 3)
    returned = lax.all_to_all(
        back.reshape(experts, capacity, width), PLANE, split_axis=0, concat_axis=0, tiled=True
    ).reshape(slot_count, width)
    mixed = jnp.zeros((rows_dev, width), jnp.float32)
    for k in range(TOP):
        result = jnp.dot(
            picks_k[k].astype(jnp.bfloat16), returned, preferred_element_type=jnp.float32
        )
        mixed = mixed + route_weight[:, k][:, None] * result
    return mixed.astype(jnp.bfloat16)


def solution(mesh):
    fine = Mesh(mesh.devices.reshape(SHAPE), NAMES)
    expert, hidden = ("xl", "y", "core"), ("z", "xh")
    in_specs = (
        P(expert, hidden),
        P(expert, None),
        P(expert, None),
        P(expert, None, hidden),
        P(expert, None, hidden),
        P(expert, hidden, None),
    )
    return jax.shard_map(
        on_device, mesh=fine, in_specs=in_specs, out_specs=P(expert, hidden), check_vma=False
    )
```
